1024 devices in a mesh: seg: 16 (over x, core), blk: 64 (over z, y).
Axes of the slice: x: 8, y: 8, z: 8, core: 2. Of those that a mesh axis runs over, the one named last changes fastest.
Arguments:
- vel_forward: float32 [81, 524288], P(None, ('seg', 'blk')), may hold values from -0.4 to 0.4
- vel_increment: float32 [81, 524288], P(None, ('seg', 'blk')), may hold values from -0.4 to 0.4
- vel_adjoint: float32 [81, 524288], P(None, ('seg', 'blk')), may hold values from -0.4 to 0.4
- vel_incr_adjoint: float32 [81, 524288], P(None, ('seg', 'blk')), may hold values from -0.4 to 0.4
- pressure_incr: float32 [4, 524288], P(None, ('seg', 'blk')), may hold values from -1.6 to 1.6
- visc_factor: float32 [27, 524288], P(None, ('seg', 'blk')), may hold values from 0.3 to 3
- octant_scale: float32 [524288], P(('seg', 'blk')), may hold values from 1 to 4
- log_visc: float32 [32768], P('blk'), may hold values from -3 to 3
- visc_direction: float32 [32768], P('blk'), may hold values from -6 to 6
- adjacency: int32 [6, 524288], P(None, ('seg', 'blk')), may hold values from -64 to 64, as said below
- hanging: int32 [6, 524288], P(None, ('seg', 'blk')), may hold values 0 or 1
- owner_map: int32 [524288], P(('seg', 'blk')), may hold values from 0 to 32767
Outputs:
- residual: float32 [81, 524288], P(None, ('seg', 'blk'))
- hessian: float32 [32768], P('blk')
The draws below stay inside these ranges and needn't reach their ends.
Inputs may be any that keep to these rules, and one draw needn't show every extreme that they name: `adjacency`: every nonzero entry points to an octant inside the window; some neighbours lie exactly 64 positions ahead and some exactly 64 behind; the boundary mark 0 occurs.
All inputs are finite; a program needn't handle non-finite values. No bound on the sum of `hanging` on one device may be relied on, other than what follows from the above.
Results may differ from the reference program's by a relative error of at most 0.0003.
Values sent between devices are 32-bit elements; how exact they have to be, the bound alone decides.
A program may use at most 32 MiB of HBM per device.

```python
import math
import jax
import jax.numpy as jnp
import numpy as np
from jax import lax

OCT_DEV = 512
HALO = 64
OCTANTS = 524288
PARAMS = 32768


def draw_adjacency(key, part):
    key = jax.random.fold_in(key, 11)
    key_size, key_sign = jax.random.split(key)
    octant = jnp.arange(OCTANTS, dtype=jnp.int32)
    reach = jax.random.randint(key_size, (6, OCTANTS), 1, HALO + 1)
    far_up = (octant % 128 == 5)[None, :]
    far_down = (octant % 128 == 69)[None, :]
    reach = jnp.where(far_up | far_down, HALO, reach)
    reach = jnp.where((octant == OCTANTS - 2)[None, :], 1, reach)
    upward = jax.random.randint(key_sign, (6, OCTANTS), 0, 2)
    upward = jnp.where(far_up, 1, upward)
    upward = jnp.where(far_down, 0, upward)
    upward = jnp.where((octant == 0)[None, :], 0, upward)
    upward = jnp.where((octant == OCTANTS - 2)[None, :], 1, upward)
    step = jnp.where(upward == 1, reach, -reach)
    neighbour = octant[None, :] + step
    inside = (neighbour >= 0) & (neighbour < OCTANTS)
    return jnp.where(inside, step, 0).astype(jnp.int32)


def set_ends(values, key, low, high):
    longest = values.shape.index(max(values.shape))
    spots = []
    for shift in (0, 1):
        where = [jax.random.randint(jax.random.fold_in(key, axis), (), 0, length) for axis, length in enumerate(values.shape)]
        where[longest] = (where[longest] + shift) % values.shape[longest]
        spots.append(tuple(where))
    return values.at[spots[0]].set(low).at[spots[1]].set(high)


def block_levels(own_key, extent, cuts, smallest, top_value):
    loudness = 1.0
    for dim, blocks in cuts:
        heights = jax.random.uniform(jax.random.fold_in(jax.random.fold_in(own_key, 6), dim), (blocks,), jnp.float32, smallest / len(cuts), top_value / len(cuts))
        loudness = loudness * jnp.repeat(jnp.exp(heights), extent[dim] // blocks).reshape((-1,) + (1,) * (len(extent) - 1 - dim))
    return loudness


def rank_table(count, skew):
    loads = [(1 << 20) // math.isqrt(grade ** skew) + 1 for grade in range(1, count + 1)]
    scale = 1 + sum(loads) // (1 << 30)
    return np.cumsum(np.array([max(1, weight // scale) for weight in loads]))


def skewed_ids(stream_key, shape, number_of, skew):
    listing = rank_table(number_of, skew)
    pick = jax.random.randint(jax.random.fold_in(stream_key, 1), shape, 0, int(listing[number_of - 1]))
    standing = jnp.searchsorted(jnp.asarray(listing, jnp.int32), pick, side="right")
    return jax.random.permutation(jax.random.fold_in(stream_key, 2), number_of)[standing].astype(jnp.int32)


def centred(stream_key, shape, spread, bound, cuts=(), kind=jnp.bfloat16):
    values = spread * jax.random.normal(stream_key, shape, jnp.float32)
    if cuts:
        values = values * block_levels(stream_key, shape, cuts, -0.22, 0.18)
    return jnp.clip(values, -bound, bound).astype(kind)


def setup_inputs(seed: int = 0) -> dict:
    key_list = jax.random.split(jax.random.key(seed), 13)
    return {
        "vel_forward": centred(key_list[0], (81, OCTANTS), 0.05, 0.4, ((1, 1024),), jnp.float32),
        "vel_increment": centred(key_list[1], (81, OCTANTS), 0.05, 0.4, ((1, 1024),), jnp.float32),
        "vel_adjoint": centred(key_list[2], (81, OCTANTS), 0.05, 0.4, ((1, 1024),), jnp.float32),
        "vel_incr_adjoint": centred(key_list[3], (81, OCTANTS), 0.05, 0.4, ((1, 1024),), jnp.float32),
        "pressure_incr": centred(key_list[4], (4, OCTANTS), 0.2, 1.6, ((1, 1024),), jnp.float32),
        "visc_factor": jnp.clip(jnp.exp(math.log(3.0) - 2.3025851 * jax.random.uniform(key_list[5], (27, OCTANTS), jnp.float32) ** block_levels(key_list[5], (27, OCTANTS), ((1, 1024),), -0.2, 0.2)), 0.3, 3.0),
        "octant_scale": jnp.clip(jnp.exp(math.log(4.0) - 1.3862944 * jax.random.uniform(key_list[6], (OCTANTS,), jnp.float32) ** block_levels(key_list[6], (OCTANTS,), ((0, 1024),), -0.2, 0.2)), 1.0, 4.0),
        "log_visc": centred(key_list[7], (PARAMS,), 0.5, 3.0, ((0, 64),), jnp.float32),
        "visc_direction": centred(key_list[8], (PARAMS,), 1.0, 6.0, ((0, 64),), jnp.float32),
        "adjacency": draw_adjacency(jax.random.fold_in(key_list[12], 71), 0),
        "hanging": set_ends((jax.random.randint(key_list[10], (6, OCTANTS), 0, 4) < 1).astype(jnp.int32), jax.random.fold_in(key_list[10], 1), 0, 1),
        "owner_map": set_ends(skewed_ids(key_list[11], (OCTANTS,), PARAMS, 1), jax.random.fold_in(key_list[11], 3), 0, PARAMS - 1).astype(jnp.int32),
    }


HIGH = lax.Precision.HIGHEST
BETA_REG = 1.0

def element_tables():
    gauss = np.array([-np.sqrt(0.6), 0.0, np.sqrt(0.6)])
    weights_one = np.array([5.0 / 9.0, 8.0 / 9.0, 5.0 / 9.0])
    values = np.stack([gauss * (gauss - 1.0) / 2.0, 1.0 - gauss * gauss, gauss * (gauss + 1.0) / 2.0])
    slopes = np.stack([gauss - 0.5, -2.0 * gauss, gauss + 0.5])
    gradient = np.zeros((3, 27, 27))
    quad_weight = np.zeros(27)
    coords = np.zeros((27, 3))
    for first in range(3):
        for second in range(3):
            for third in range(3):
                point = (first * 3 + second) * 3 + third
                quad_weight[point] = weights_one[first] * weights_one[second] * weights_one[third]
                coords[point] = [gauss[first], gauss[second], gauss[third]]
                for node_a in range(3):
                    for node_b in range(3):
                        for node_c in range(3):
                            node = (node_a * 3 + node_b) * 3 + node_c
                            gradient[0, point, node] = slopes[node_a, first] * values[node_b, second] * values[node_c, third]
                            gradient[1, point, node] = values[node_a, first] * slopes[node_b, second] * values[node_c, third]
                            gradient[2, point, node] = values[node_a, first] * values[node_b, second] * slopes[node_c, third]
    pairs = [(0, 0), (1, 1), (2, 2), (0, 1), (1, 2), (0, 2)]
    strain = np.zeros((162, 81))
    for comp in range(6):
        left, right = pairs[comp]
        strain[comp * 27:(comp + 1) * 27, left * 27:(left + 1) * 27] += 0.5 * gradient[right]
        strain[comp * 27:(comp + 1) * 27, right * 27:(right + 1) * 27] += 0.5 * gradient[left]
    diverge = strain[0:27] + strain[27:54] + strain[54:81]
    contract = np.repeat(np.array([1.0, 1.0, 1.0, 2.0, 2.0, 2.0]), 27)
    basis_press = np.concatenate([np.ones((27, 1)), coords], 1)
    select = np.zeros((81, 162))
    for face in range(6):
        direction = face // 2
        side = 2 * (face % 2)
        nodes = [node for node in range(27) if (node // 9, node // 3 % 3, node % 3)[direction] == side]
        for comp in range(3):
            for place in range(9):
                select[comp * 27 + nodes[place], face * 27 + comp * 9 + place] = 1.0
    return (jnp.asarray(strain, jnp.float32), jnp.asarray(diverge, jnp.float32), jnp.asarray(basis_press, jnp.float32), jnp.asarray(quad_weight, jnp.float32), jnp.asarray(contract, jnp.float32), jnp.asarray(select, jnp.float32))

def element_work(tables, velocity, pressure, factors, scale, log_oct, dir_oct):
    strain, diverge, basis_press, quad_weight, contract, select = tables
    rates = jnp.einsum('sv,kvn->ksn', strain, velocity, precision=HIGH) * scale[None, None, :]
    rate_fwd, rate_inc, rate_adj, rate_incadj = (rates[0], rates[1], rates[2], rates[3])
    jacobian = 1.0 / (scale * scale * scale)
    weighted = quad_weight[:, None] * jacobian[None, :]
    viscosity = jnp.exp(log_oct)[None, :] * factors
    coef = jnp.tile(2.0 * viscosity * weighted, (6, 1)) * contract[:, None]
    stress = coef * (rate_incadj + dir_oct[None, :] * rate_adj)
    press_quad = weighted * jnp.dot(basis_press, pressure, precision=HIGH)
    local = scale[None, :] * (jnp.dot(strain.T, stress, precision=HIGH) - jnp.dot(diverge.T, press_quad, precision=HIGH))
    contrib = coef * (rate_inc * rate_adj + rate_fwd * rate_incadj + dir_oct[None, :] * rate_fwd * rate_adj)
    grad = lax.optimization_barrier(jnp.sum(contrib, axis=0))
    face = jnp.dot(select.T, local, precision=HIGH)
    return (local, face, grad)

def assemble(tables, faces3, columns, valid, hanging):
    select = tables[5]
    width = faces3.shape[2]
    pieces = []
    for face in range(6):
        other = face ^ 1
        picked = jnp.take(faces3[other], jnp.clip(columns[face], 0, width - 1), axis=1)
        weight = jnp.where(valid[face], jnp.where(hanging[face] == 1, 0.25, 1.0), 0.0).astype(picked.dtype)
        pieces.append(picked * weight[None, :])
    return jnp.dot(select, jnp.concatenate(pieces, 0), precision=HIGH)

def laplace(field):
    padded = jnp.pad(field, 1)
    return 2.0 * field - padded[:-2] - padded[2:]

def reference(vel_forward, vel_increment, vel_adjoint, vel_incr_adjoint, pressure_incr, visc_factor, octant_scale, log_visc, visc_direction, adjacency, hanging, owner_map):
    tables = element_tables()
    log_oct = jnp.take(log_visc, owner_map)
    dir_oct = jnp.take(visc_direction, owner_map)
    velocity = jnp.stack([vel_forward, vel_increment, vel_adjoint, vel_incr_adjoint])
    blocks = OCTANTS // OCT_DEV

    def one_block(index):
        begin = (index * OCT_DEV).astype(jnp.int32)
        return element_work(tables, lax.dynamic_slice_in_dim(velocity, begin, OCT_DEV, 2), lax.dynamic_slice_in_dim(pressure_incr, begin, OCT_DEV, 1), lax.dynamic_slice_in_dim(visc_factor, begin, OCT_DEV, 1), lax.dynamic_slice_in_dim(octant_scale, begin, OCT_DEV, 0), lax.dynamic_slice_in_dim(log_oct, begin, OCT_DEV, 0), lax.dynamic_slice_in_dim(dir_oct, begin, OCT_DEV, 0))
    local_b, face_b, grad_b = lax.map(one_block, jnp.arange(blocks, dtype=jnp.int32))
    local = jnp.transpose(local_b, (1, 0, 2)).reshape(81, OCTANTS)
    face = jnp.transpose(face_b, (1, 0, 2)).reshape(162, OCTANTS)
    grad = grad_b.reshape(OCTANTS)
    positions = jnp.arange(OCTANTS, dtype=jnp.int32)
    columns = positions[None, :] + adjacency
    residual = local + assemble(tables, face.reshape(6, 27, OCTANTS), columns, adjacency != 0, hanging)
    summed = jax.ops.segment_sum(grad, owner_map, num_segments=PARAMS)
    hessian = summed + BETA_REG * laplace(visc_direction)
    return (residual, hessian)
```

```python
import functools

import jax
import jax.numpy as jnp
import ml_dtypes
import numpy as np
from jax import lax
from jax.experimental import pallas as pl
from jax.experimental.pallas import tpu as pltpu
from jax.sharding import PartitionSpec as P

MESH = pl.DeviceIdType.MESH
F32 = jnp.float32
BF16 = jnp.bfloat16
BETA_REG = 1.0
SHEAR = (1.0, 1.0, 1.0, 2.0, 2.0, 2.0)


def element_tables():
    gauss = np.array([-np.sqrt(0.6), 0.0, np.sqrt(0.6)])
    weights_one = np.array([5.0 / 9.0, 8.0 / 9.0, 5.0 / 9.0])
    values = np.stack([gauss * (gauss - 1.0) / 2.0, 1.0 - gauss * gauss, gauss * (gauss + 1.0) / 2.0])
    slopes = np.stack([gauss - 0.5, -2.0 * gauss, gauss + 0.5])
    gradient = np.zeros((3, 27, 27))
    for r in range(3):
        parts = [slopes if d == r else values for d in range(3)]
        gradient[r] = np.einsum("ia,jb,kc->abcijk", *parts).reshape(27, 27)
    quad_weight = np.einsum("a,b,c->abc", weights_one, weights_one, weights_one).reshape(27)
    coords = np.stack([g.reshape(27) for g in np.meshgrid(gauss, gauss, gauss, indexing="ij")], 1)
    pairs = [(0, 0), (1, 1), (2, 2), (0, 1), (1, 2), (0, 2)]
    strain = np.zeros((6, 27, 81))
    for comp, (left, right) in enumerate(pairs):
        strain[comp, :, left * 27 : (left + 1) * 27] += 0.5 * gradient[right]
        strain[comp, :, right * 27 : (right + 1) * 27] += 0.5 * gradient[left]
    select = np.zeros((81, 6, 32))
    for face in range(6):
        direction, side = face // 2, 2 * (face % 2)
        nodes = [n for n in range(27) if (n // 9, n // 3 % 3, n % 3)[direction] == side]
        for comp in range(3):
            for place in range(9):
                select[comp * 27 + nodes[place], face, comp * 9 + place] = 1.0
    return strain.astype(np.float32), quad_weight, coords, select


def halves(table):
    high = table.astype(ml_dtypes.bfloat16)
    low = (table - high.astype(np.float32)).astype(ml_dtypes.bfloat16)
    return high, low


def constants():
    strain, quad_weight, coords, select = element_tables()
    padded = np.zeros((6, 32, 81), np.float32)
    padded[:, :27] = strain
    padded = padded.reshape(192, 81)
    high, low = halves(padded)
    rate = np.zeros((192, 256), ml_dtypes.bfloat16)
    rate[:, 0:80], rate[:, 80:160], rate[:, 160:240] = high[:, :80], high[:, :80], low[:, :80]
    rate[:, 240], rate[:, 241], rate[:, 242] = high[:, 80], high[:, 80], low[:, 80]
    rows = np.zeros((288, 192), np.float32)
    rows[:81] = padded.T
    rows[88:280] = select.reshape(81, 192).T @ padded.T
    high, low = halves(rows)
    force = np.concatenate([high, high, low], 1)
    place = np.zeros((96, 384), ml_dtypes.bfloat16)
    place[:81, :192] = select.reshape(81, 192)
    place[:81, 192:] = select.reshape(81, 192)
    points = np.zeros((4, 32, 128), np.float32)
    points[0, :27] = quad_weight[:, None]
    for d in range(3):
        points[d + 1, :27] = coords[:, d, None]
    return rate, force, place, points


def split(x):
    high = x.astype(BF16)
    return high, (x - high.astype(F32)).astype(BF16)


def iota(shape, dim):
    return lax.broadcasted_iota(jnp.int32, shape, dim)


def kernel(
    nz, ny, nseg,
    vel_f, vel_i, vel_a, vel_ia, press_h, visc_h, scale_h, log_h, dir_h, adj_h, hang_h, own_h,
    rate_h, force_h, place_h, points_h,
    res_out, hess_out,
    vel, press, visc, scale, log_v, dir_v, adj, hang, own, rate, force, place, points,
    rates, vstack, keys, table, side, onehot, sums, reply, gathered, partial, faces, halo, hits,
    stress, local, spread, picked, res, hess,
    load_sem, out_sem, key_send, key_recv, tab_send, tab_recv, side_send, side_recv,
    sum_send, sum_recv, rep_send, rep_recv, par_send, par_recv, halo_send, halo_recv,
):
    seg, blk = lax.axis_index("seg"), lax.axis_index("blk")
    z, y = blk // ny, lax.rem(blk, ny)
    nblk = nz * ny
    flat = seg * nblk + blk
    total = nseg * nblk
    after, before = lax.rem(flat + 1, total), lax.rem(flat + total - 1, total)
    after, before = (after // nblk, lax.rem(after, nblk)), (before // nblk, lax.rem(before, nblk))
    z_peer = [(seg, lax.rem(z + k, nz) * ny + y) for k in range(nz)]
    y_peer = [(seg, z * ny + lax.rem(y + k, ny)) for k in range(ny)]
    s_peer = [(lax.rem(seg + k, nseg), blk) for k in range(nseg)]

    pairs = [
        (vel_f, vel.at[0]), (vel_i, vel.at[1]), (vel_a, vel.at[2]), (vel_ia, vel.at[3]), (rate_h, rate), (visc_h, visc),
        (scale_h, scale), (own_h, own), (points_h, points), (log_h, log_v), (dir_h, dir_v), (adj_h, adj), (hang_h, hang),
        (force_h, force), (press_h, press), (place_h, place),
    ]
    loads = [pltpu.make_async_copy(a, b, load_sem.at[i]) for i, (a, b) in enumerate(pairs)]
    for load in loads:
        load.start()

    barrier = pltpu.get_barrier_semaphore()
    peers = z_peer[1:] + y_peer[1:] + [after, before] + s_peer[1:]
    for peer in peers:
        pl.semaphore_signal(barrier, inc=1, device_id=peer, device_id_type=MESH)

    def send(src, dst, send_sem, recv_sem, peer):
        pltpu.make_async_remote_copy(
            src_ref=src, dst_ref=dst, send_sem=send_sem, recv_sem=recv_sem, device_id=peer, device_id_type=MESH
        ).start()

    def drain(ref, sem):
        pltpu.make_async_copy(ref, ref, sem).wait()

    for i in range(4):
        loads[i].wait()
        if i == 0:
            loads[4].wait()
        high, low = split(vel[i, 0:80, :])
        last_high = vel[i, 80:81, :].astype(BF16).astype(F32)
        last_low = vel[i, 80:81, :] - last_high
        row = iota((16, 512), 0)
        tail = jnp.where((row == 0) | (row == 2), last_high, jnp.where(row == 1, last_low, 0.0)).astype(BF16)
        vstack[0:80, :] = high
        vstack[80:160, :] = low
        vstack[160:240, :] = high
        vstack[240:256, :] = tail
        rates[i] = jnp.dot(rate[...], vstack[...], preferred_element_type=F32)

    for i in range(5, 9):
        loads[i].wait()
    inverse = 1.0 / scale[...]
    factor = jnp.concatenate([visc[...], jnp.zeros((5, 512), F32)], 0)
    base = 2.0 * factor * points[0][:, 0:1] * inverse
    first = jnp.zeros((32, 512), F32)
    second = jnp.zeros((32, 512), F32)
    for c in range(6):
        at = pl.ds(32 * c, 32)
        fwd, inc, adjoint, incadj = rates[0, at, :], rates[1, at, :], rates[2, at, :], rates[3, at, :]
        first += SHEAR[c] * (inc * adjoint + fwd * incadj)
        second += SHEAR[c] * (fwd * adjoint)
    sum_first = jnp.sum(base * first, axis=0, keepdims=True)
    sum_second = jnp.sum(base * second, axis=0, keepdims=True)
    owner = own[...]
    row_of = owner // 128
    block_of = row_of // 4
    block_y = lax.rem(block_of, ny)
    slot = lax.rem(y - block_y + ny, ny)
    key = (block_of // ny) * (4 * ny) + slot * 4 + lax.rem(row_of, 4)
    column = lax.rem(owner, 128)
    keys[0, 0:1, :] = key.astype(F32)
    keys[0, 1:2, :] = column.astype(F32)
    keys[0, 2:3, :] = sum_first
    keys[0, 3:4, :] = sum_second
    loads[9].wait()
    loads[10].wait()
    table[0, 0:4, :] = log_v[...]
    table[0, 4:8, :] = dir_v[...]

    pl.semaphore_wait(barrier, len(peers))
    for k in range(1, nz):
        send(keys.at[0], keys.at[k], key_send, key_recv, z_peer[k])
    for k in range(1, ny):
        send(table.at[0], table.at[k], tab_send, tab_recv, y_peer[k])
    send(table.at[0], side.at[0], side_send.at[0], side_recv.at[0], after)
    send(table.at[0], side.at[1], side_send.at[1], side_recv.at[1], before)

    loads[11].wait()
    loads[12].wait()
    lane = lax.rem(iota((1, 512), 1), 128)
    for f in range(6):
        reach = adj[f : f + 1, :]
        target = lax.rem(lane + reach + 384, 256)
        weight = jnp.where(reach != 0, jnp.where(hang[f : f + 1, :] == 1, 0.25, 1.0), 0.0)
        hits[f] = jnp.where(iota((256, 512), 0) == target, weight, 0.0).astype(BF16)

    drain(keys.at[pl.ds(0, nz - 1)], key_recv)
    rho = iota((8 * ny, 512), 0)
    wanted = (z * (4 * ny) + (rho // 8) * 4 + lax.rem(rho, 4)).astype(F32)
    is_second = lax.rem(rho, 8) >= 4
    acc = jnp.zeros((16 * ny, 128), F32)
    for d in range(nz):
        hit = keys[d, 0:1, :] == wanted
        value = jnp.where(is_second, keys[d, 3:4, :], keys[d, 2:3, :])
        value = jnp.where(hit, value, 0.0)
        high, low = split(value)
        onehot[d] = jnp.where(iota((128, 512), 0).astype(F32) == keys[d, 1:2, :], 1.0, 0.0).astype(BF16)
        acc += lax.dot_general(
            jnp.concatenate([high, low], 0), onehot[d], (((1,), (1,)), ((), ())), preferred_element_type=F32
        )
    dense = acc[0 : 8 * ny, :] + acc[8 * ny : 16 * ny, :]
    for k in range(ny):
        sums[0, k] = dense[8 * k : 8 * k + 8, :]
    for k in range(1, ny):
        send(sums.at[0, k], sums.at[1, k], sum_send, sum_recv, y_peer[ny - k])

    drain(table.at[pl.ds(0, ny - 1)], tab_recv)
    row = iota((8 * ny, 512), 0)
    for part in range(2):
        rows = jnp.concatenate([table[k, 4 * part : 4 * part + 4, :] for k in range(ny)], 0)
        high, low = split(rows)
        spread[part] = jnp.concatenate([high, low], 0)
    key_row = z * (4 * ny) + lax.rem(iota((8 * ny, 512), 0), 4 * ny)
    for d in range(nz):
        pick = jnp.where(keys[d, 0:1, :] == key_row.astype(F32), 1.0, 0.0).astype(BF16)
        mask = onehot[d].astype(F32)
        for part in range(2):
            found = lax.dot_general(spread[part], pick, (((0,), (0,)), ((), ())), preferred_element_type=F32)
            answer = jnp.sum(found * mask, axis=0, keepdims=True)
            reply[d, part : part + 1, :] = answer
    for d in range(1, nz):
        send(reply.at[d], gathered.at[d], rep_send, rep_recv, z_peer[nz - d])

    drain(sums.at[1, pl.ds(0, ny - 1)], sum_recv)
    mine = sums[0, 0]
    for k in range(1, ny):
        mine += sums[1, k]
    share = jnp.exp(table[0, 0:4, :]) * (mine[0:4, :] + table[0, 4:8, :] * mine[4:8, :])
    partial[seg] = share
    for k in range(1, nseg):
        send(partial.at[seg], partial.at[seg], par_send, par_recv, s_peer[k])

    drain(gathered.at[pl.ds(0, nz - 1)], rep_recv)
    found = reply[0]
    for k in range(1, nz):
        found += gathered[k]
    viscosity = jnp.exp(found[0:1, :]) * base
    direction = found[1:2, :]
    for i in range(13, 16):
        loads[i].wait()
    pressure = (
        press[0:1, :] + points[1][:, 0:1] * press[1:2, :] + points[2][:, 0:1] * press[2:3, :]
        + points[3][:, 0:1] * press[3:4, :]
    ) * points[0][:, 0:1] * (inverse * inverse)
    for c in range(6):
        at = pl.ds(32 * c, 32)
        value = SHEAR[c] * viscosity * (rates[3, at, :] + direction * rates[2, at, :])
        if c < 3:
            value -= pressure
        high, low = split(value)
        stress[32 * c : 32 * c + 32, :] = high
        stress[192 + 32 * c : 224 + 32 * c, :] = low
        stress[384 + 32 * c : 416 + 32 * c, :] = high
    local[...] = jnp.dot(force[...], stress[...], preferred_element_type=F32)
    for b in range(4):
        faces[b] = local[88:280, 128 * b : 128 * b + 128]
    send(faces.at[3], halo.at[0], halo_send.at[0], halo_recv.at[0], after)
    send(faces.at[0], halo.at[1], halo_send.at[1], halo_recv.at[1], before)

    low_lane = iota((192, 128), 1) < 64

    def window(b):
        last = halo[0] if b == 0 else faces[b - 1]
        following = halo[1] if b == 3 else faces[b + 1]
        beside_high, beside_low = split(jnp.where(low_lane, following, last))
        own_high, own_low = split(faces[b])
        for f in range(6):
            at = slice(32 * f, 32 * f + 32)
            window_rows = jnp.concatenate([
                jnp.concatenate([beside_high[at], own_high[at]], 1),
                jnp.concatenate([beside_low[at], own_low[at]], 1),
            ], 0)
            other = f ^ 1
            got = jnp.dot(window_rows, hits[other, :, 128 * b : 128 * b + 128], preferred_element_type=F32)
            picked[32 * other : 32 * other + 32, 128 * b : 128 * b + 128] = got[0:32].astype(BF16)
            picked[192 + 32 * other : 224 + 32 * other, 128 * b : 128 * b + 128] = got[32:64].astype(BF16)

    window(1)
    window(2)
    drain(halo.at[0], halo_recv.at[0])
    window(0)
    drain(halo.at[1], halo_recv.at[1])
    window(3)
    added = jnp.dot(place[...], picked[...], preferred_element_type=F32)
    res[...] = local[0:81, :] + added[0:81, :]
    out_res = pltpu.make_async_copy(res, res_out, out_sem.at[0])
    out_res.start()

    drain(side.at[0], side_recv.at[0])
    drain(side.at[1], side_recv.at[1])
    tile = table[0]
    row, lane = iota((8, 128), 0), iota((8, 128), 1)
    up = pltpu.roll(tile, 1, 1)
    up_row = pltpu.roll(up, 1, 0)
    up_side = pltpu.roll(pltpu.roll(side[0], 1, 1), 5, 0)
    up_side = jnp.where(blk == 0, 0.0, up_side)
    prev = jnp.where(lane == 0, jnp.where(row == 4, up_side, up_row), up)
    down = pltpu.roll(tile, 127, 1)
    down_row = pltpu.roll(down, 7, 0)
    down_side = pltpu.roll(pltpu.roll(side[1], 127, 1), 3, 0)
    down_side = jnp.where(blk == nblk - 1, 0.0, down_side)
    following = jnp.where(lane == 127, jnp.where(row == 7, down_side, down_row), down)
    smooth = BETA_REG * (2.0 * tile - prev - following)

    drain(partial.at[pl.ds(0, nseg - 1)], par_recv)
    result = partial[0]
    for k in range(1, nseg):
        result += partial[k]
    hess[...] = result + smooth[4:8, :]
    out_hess = pltpu.make_async_copy(hess, hess_out, out_sem.at[1])
    out_hess.start()

    drain(keys.at[pl.ds(0, nz - 1)], key_send)
    drain(table.at[pl.ds(0, ny - 1)], tab_send)
    drain(sums.at[1, pl.ds(0, ny - 1)], sum_send)
    drain(gathered.at[pl.ds(0, nz - 1)], rep_send)
    drain(partial.at[pl.ds(0, nseg - 1)], par_send)
    for i in range(2):
        drain(side.at[i], side_send.at[i])
        drain(halo.at[i], halo_send.at[i])
    out_res.wait()
    out_hess.wait()


def per_device(nz, ny, nseg, tables, *args):
    vel = args[:4]
    press, visc, scale, log_visc, direction, adj, hang, owner = args[4:]
    dma = pltpu.SemaphoreType.DMA
    vmem = pltpu.VMEM
    residual, hessian = pl.pallas_call(
        functools.partial(kernel, nz, ny, nseg),
        out_shape=(jax.ShapeDtypeStruct((81, 512), F32), jax.ShapeDtypeStruct((4, 128), F32)),
        in_specs=[pl.BlockSpec(memory_space=pl.ANY)] * 16,
        out_specs=(pl.BlockSpec(memory_space=pl.ANY),) * 2,
        scratch_shapes=[
            vmem((4, 81, 512), F32), vmem((4, 512), F32), vmem((27, 512), F32), vmem((1, 512), F32),
            vmem((4, 128), F32), vmem((4, 128), F32), vmem((6, 512), jnp.int32), vmem((6, 512), jnp.int32),
            vmem((1, 512), jnp.int32),
            vmem((192, 256), BF16), vmem((288, 576), BF16), vmem((96, 384), BF16), vmem((4, 32, 128), F32),
            vmem((4, 192, 512), F32),
            vmem((256, 512), BF16),
            vmem((nz, 4, 512), F32),
            vmem((ny, 8, 128), F32),
            vmem((2, 8, 128), F32),
            vmem((nz, 128, 512), BF16),
            vmem((2, ny, 8, 128), F32),
            vmem((nz, 2, 512), F32),
            vmem((nz, 2, 512), F32),
            vmem((nseg, 4, 128), F32),
            vmem((4, 192, 128), F32),
            vmem((2, 192, 128), F32),
            vmem((6, 256, 512), BF16),
            vmem((576, 512), BF16),
            vmem((288, 512), F32),
            vmem((2, 8 * ny, 128), BF16),
            vmem((384, 512), BF16),
            vmem((81, 512), F32), vmem((4, 128), F32),
            dma((16,)), dma((2,)), dma, dma, dma, dma, dma((2,)), dma((2,)),
            dma, dma, dma, dma, dma, dma, dma((2,)), dma((2,)),
        ],
        compiler_params=pltpu.CompilerParams(
            collective_id=0, has_side_effects=True, vmem_limit_bytes=32 * 1024 * 1024
        ),
    )(
        *vel, press, visc, scale.reshape(1, 512), log_visc.reshape(4, 128), direction.reshape(4, 128), adj, hang,
        owner.reshape(1, 512), *tables,
    )
    return residual, hessian.reshape(512)


def solution(mesh):
    nseg, nblk = mesh.shape["seg"], mesh.shape["blk"]
    ny = max(d for d in (1, 2, 4, 8) if d * d <= nblk)
    tables = constants()
    octants = P(None, ("seg", "blk"))
    line = P(("seg", "blk"))
    placed = (octants,) * 6 + (line, P("blk"), P("blk"), octants, octants, line)

    def step(*args):
        return per_device(nblk // ny, ny, nseg, [jnp.asarray(t) for t in tables], *args)

    return jax.shard_map(step, mesh=mesh, in_specs=placed, out_specs=(octants, P("blk")), check_vma=False)
```

```python
import functools

import jax
import jax.numpy as jnp
import ml_dtypes
import numpy as np
from jax import lax
from jax.experimental import pallas as pl
from jax.experimental.pallas import tpu as pltpu
from jax.sharding import PartitionSpec as P

MESH = pl.DeviceIdType.MESH
F32 = jnp.float32
BF16 = jnp.bfloat16
BETA_REG = 1.0
SHEAR = (1.0, 1.0, 1.0, 2.0, 2.0, 2.0)


def element_tables():
    gauss = np.array([-np.sqrt(0.6), 0.0, np.sqrt(0.6)])
    weights_one = np.array([5.0 / 9.0, 8.0 / 9.0, 5.0 / 9.0])
    values = np.stack([gauss * (gauss - 1.0) / 2.0, 1.0 - gauss * gauss, gauss * (gauss + 1.0) / 2.0])
    slopes = np.stack([gauss - 0.5, -2.0 * gauss, gauss + 0.5])
    gradient = np.zeros((3, 27, 27))
    for r in range(3):
        parts = [slopes if d == r else values for d in range(3)]
        gradient[r] = np.einsum("ia,jb,kc->abcijk", *parts).reshape(27, 27)
    quad_weight = np.einsum("a,b,c->abc", weights_one, weights_one, weights_one).reshape(27)
    coords = np.stack([g.reshape(27) for g in np.meshgrid(gauss, gauss, gauss, indexing="ij")], 1)
    pairs = [(0, 0), (1, 1), (2, 2), (0, 1), (1, 2), (0, 2)]
    strain = np.zeros((6, 27, 81))
    for comp, (left, right) in enumerate(pairs):
        strain[comp, :, left * 27 : (left + 1) * 27] += 0.5 * gradient[right]
        strain[comp, :, right * 27 : (right + 1) * 27] += 0.5 * gradient[left]
    select = np.zeros((81, 6, 32))
    for face in range(6):
        direction, side = face // 2, 2 * (face % 2)
        nodes = [n for n in range(27) if (n // 9, n // 3 % 3, n % 3)[direction] == side]
        for comp in range(3):
            for place in range(9):
                select[comp * 27 + nodes[place], face, comp * 9 + place] = 1.0
    return strain.astype(np.float32), quad_weight, coords, select


def halves(table):
    high = table.astype(ml_dtypes.bfloat16)
    low = (table - high.astype(np.float32)).astype(ml_dtypes.bfloat16)
    return high, low


def constants():
    strain, quad_weight, coords, select = element_tables()
    padded = np.zeros((6, 32, 81), np.float32)
    padded[:, :27] = strain
    padded = padded.reshape(192, 81)
    high, low = halves(padded)
    rate = np.zeros((192, 256), ml_dtypes.bfloat16)
    rate[:, 0:80], rate[:, 80:160], rate[:, 160:240] = high[:, :80], high[:, :80], low[:, :80]
    rate[:, 240], rate[:, 241], rate[:, 242] = high[:, 80], high[:, 80], low[:, 80]
    rows = np.zeros((288, 192), np.float32)
    rows[:81] = padded.T
    rows[88:280] = select.reshape(81, 192).T @ padded.T
    high, low = halves(rows)
    force = np.concatenate([high, high, low], 1)
    place = np.zeros((96, 384), ml_dtypes.bfloat16)
    place[:81, :192] = select.reshape(81, 192)
    place[:81, 192:] = select.reshape(81, 192)
    points = np.zeros((4, 32, 128), np.float32)
    points[0, :27] = quad_weight[:, None]
    for d in range(3):
        points[d + 1, :27] = coords[:, d, None]
    return rate, force, place, points


def split(x):
    high = x.astype(BF16)
    return high, (x - high.astype(F32)).astype(BF16)


def iota(shape, dim):
    return lax.broadcasted_iota(jnp.int32, shape, dim)


def far_first(count, stride):
    return sorted(range(1, count), key=lambda k: -min(k // stride, (count - k) // stride))


def kernel(
    nz, ny, nseg,
    vel_f, vel_i, vel_a, vel_ia, press_h, visc_h, scale_h, log_h, dir_h, adj_h, hang_h, own_h,
    rate_h, force_h, place_h, points_h,
    res, hess,
    vel, press, visc, scale, log_v, dir_v, adj, hang, own, rate, force, place, points,
    rates, vstack, keys, table, side, onehot, sums, reply, gathered, partial, faces, halo, hits,
    stress, local, spread, picked,
    load_sem, key_send, key_recv, tab_send, tab_recv, side_send, side_recv,
    sum_send, sum_recv, rep_send, rep_recv, par_send, par_recv, halo_send, halo_recv,
):
    seg, blk = lax.axis_index("seg"), lax.axis_index("blk")
    z, y = blk // ny, lax.rem(blk, ny)
    nblk = nz * ny
    flat = seg * nblk + blk
    total = nseg * nblk
    after, before = lax.rem(flat + 1, total), lax.rem(flat + total - 1, total)
    after, before = (after // nblk, lax.rem(after, nblk)), (before // nblk, lax.rem(before, nblk))
    z_peer = [(seg, lax.rem(z + k, nz) * ny + y) for k in range(nz)]
    y_peer = [(seg, z * ny + lax.rem(y + k, ny)) for k in range(ny)]
    s_peer = [(lax.rem(seg + k, nseg), blk) for k in range(nseg)]

    pairs = [
        (vel_f, vel.at[0]), (vel_i, vel.at[1]), (vel_a, vel.at[2]), (vel_ia, vel.at[3]), (rate_h, rate), (visc_h, visc),
        (scale_h, scale), (own_h, own), (points_h, points), (log_h, log_v), (dir_h, dir_v), (adj_h, adj), (hang_h, hang),
        (force_h, force), (press_h, press), (place_h, place),
    ]
    loads = [pltpu.make_async_copy(a, b, load_sem.at[i]) for i, (a, b) in enumerate(pairs)]
    for load in loads:
        load.start()

    barrier = pltpu.get_barrier_semaphore()
    near_s = [k for k in range(1, nseg) if k in (1, 2, 3, nseg - 3, nseg - 2, nseg - 1)]
    near_y = [k for k in range(1, ny) if k in (1, ny - 1)]
    peers = [y_peer[k] for k in near_y] + [s_peer[k] for k in near_s] + z_peer[1:]
    peers += [y_peer[k] for k in range(1, ny) if k not in near_y] + [after, before]
    peers += [s_peer[k] for k in range(1, nseg) if k not in near_s]
    for peer in peers:
        pl.semaphore_signal(barrier, inc=1, device_id=peer, device_id_type=MESH)

    def send(src, dst, send_sem, recv_sem, peer):
        pltpu.make_async_remote_copy(
            src_ref=src, dst_ref=dst, send_sem=send_sem, recv_sem=recv_sem, device_id=peer, device_id_type=MESH
        ).start()

    def drain(ref, sem):
        pltpu.make_async_copy(ref, ref, sem).wait()

    for i in range(4):
        loads[i].wait()
        if i == 0:
            loads[4].wait()
        high, low = split(vel[i, 0:80, :])
        last_high = vel[i, 80:81, :].astype(BF16).astype(F32)
        last_low = vel[i, 80:81, :] - last_high
        row = iota((16, 512), 0)
        tail = jnp.where((row == 0) | (row == 2), last_high, jnp.where(row == 1, last_low, 0.0)).astype(BF16)
        vstack[0:80, :] = high
        vstack[80:160, :] = low
        vstack[160:240, :] = high
        vstack[240:256, :] = tail
        rates[i] = jnp.dot(rate[...], vstack[...], preferred_element_type=F32)

    for i in range(5, 9):
        loads[i].wait()
    inverse = 1.0 / scale[...]
    factor = jnp.concatenate([visc[...], jnp.zeros((5, 512), F32)], 0)
    base = 2.0 * factor * points[0][:, 0:1] * inverse
    first = jnp.zeros((32, 512), F32)
    second = jnp.zeros((32, 512), F32)
    for c in range(6):
        at = pl.ds(32 * c, 32)
        fwd, inc, adjoint, incadj = rates[0, at, :], rates[1, at, :], rates[2, at, :], rates[3, at, :]
        first += SHEAR[c] * (inc * adjoint + fwd * incadj)
        second += SHEAR[c] * (fwd * adjoint)
    sum_first = jnp.sum(base * first, axis=0, keepdims=True)
    sum_second = jnp.sum(base * second, axis=0, keepdims=True)
    owner = own[...]
    row_of = owner // 128
    block_of = row_of // 4
    block_y = lax.rem(block_of, ny)
    slot = lax.rem(y - block_y + ny, ny)
    key = (block_of // ny) * (4 * ny) + slot * 4 + lax.rem(row_of, 4)
    column = lax.rem(owner, 128)
    keys[0, 0:1, :] = key.astype(F32)
    keys[0, 1:2, :] = column.astype(F32)
    keys[0, 2:3, :] = sum_first
    keys[0, 3:4, :] = sum_second
    loads[9].wait()
    loads[10].wait()
    table[0, 0:4, :] = log_v[...]
    table[0, 4:8, :] = dir_v[...]

    pl.semaphore_wait(barrier, len(peers))
    for k in range(1, nz):
        send(keys.at[0], keys.at[k], key_send, key_recv.at[k], z_peer[k])
    for k in range(1, ny):
        send(table.at[0], table.at[k], tab_send, tab_recv, y_peer[k])
    send(table.at[0], side.at[0], side_send.at[0], side_recv.at[0], after)
    send(table.at[0], side.at[1], side_send.at[1], side_recv.at[1], before)

    loads[11].wait()
    loads[12].wait()
    lane = lax.rem(iota((1, 512), 1), 128)
    for f in range(6):
        reach = adj[f : f + 1, :]
        target = lax.rem(lane + reach + 384, 256)
        weight = jnp.where(reach != 0, jnp.where(hang[f : f + 1, :] == 1, 0.25, 1.0), 0.0)
        hits[f] = jnp.where(iota((256, 512), 0) == target, weight, 0.0).astype(BF16)

    rho = iota((8 * ny, 512), 0)
    wanted = (z * (4 * ny) + (rho // 8) * 4 + lax.rem(rho, 4)).astype(F32)
    is_second = lax.rem(rho, 8) >= 4
    acc = jnp.zeros((16 * ny, 128), F32)
    for d in [0] + list(range(nz - 1, 0, -1)):
        if d > 0:
            drain(keys.at[d], key_recv.at[d])
        hit = keys[d, 0:1, :] == wanted
        value = jnp.where(is_second, keys[d, 3:4, :], keys[d, 2:3, :])
        value = jnp.where(hit, value, 0.0)
        high, low = split(value)
        onehot[d] = jnp.where(iota((128, 512), 0).astype(F32) == keys[d, 1:2, :], 1.0, 0.0).astype(BF16)
        acc += lax.dot_general(
            jnp.concatenate([high, low], 0), onehot[d], (((1,), (1,)), ((), ())), preferred_element_type=F32
        )
    dense = acc[0 : 8 * ny, :] + acc[8 * ny : 16 * ny, :]
    for k in range(ny):
        sums[0, k] = dense[8 * k : 8 * k + 8, :]
    for k in far_first(ny, 1):
        send(sums.at[0, k], sums.at[1, k], sum_send, sum_recv, y_peer[ny - k])

    drain(table.at[pl.ds(0, ny - 1)], tab_recv)
    row = iota((8 * ny, 512), 0)
    for part in range(2):
        rows = jnp.concatenate([table[k, 4 * part : 4 * part + 4, :] for k in range(ny)], 0)
        high, low = split(rows)
        spread[part] = jnp.concatenate([high, low], 0)
    key_row = z * (4 * ny) + lax.rem(iota((8 * ny, 512), 0), 4 * ny)
    for d in range(nz):
        pick = jnp.where(keys[d, 0:1, :] == key_row.astype(F32), 1.0, 0.0).astype(BF16)
        mask = onehot[d].astype(F32)
        for part in range(2):
            found = lax.dot_general(spread[part], pick, (((0,), (0,)), ((), ())), preferred_element_type=F32)
            answer = jnp.sum(found * mask, axis=0, keepdims=True)
            reply[d, part : part + 1, :] = answer
    for d in range(1, nz):
        send(reply.at[d], gathered.at[d], rep_send, rep_recv, z_peer[nz - d])

    drain(sums.at[1, pl.ds(0, ny - 1)], sum_recv)
    mine = sums[0, 0]
    for k in range(1, ny):
        mine += sums[1, k]
    share = jnp.exp(table[0, 0:4, :]) * (mine[0:4, :] + table[0, 4:8, :] * mine[4:8, :])
    partial[seg] = share
    for k in far_first(nseg, 2):
        send(partial.at[seg], partial.at[seg], par_send, par_recv, s_peer[k])

    drain(gathered.at[pl.ds(0, nz - 1)], rep_recv)
    found = reply[0]
    for k in range(1, nz):
        found += gathered[k]
    viscosity = jnp.exp(found[0:1, :]) * base
    direction = found[1:2, :]
    for i in range(13, 16):
        loads[i].wait()
    pressure = (
        press[0:1, :] + points[1][:, 0:1] * press[1:2, :] + points[2][:, 0:1] * press[2:3, :]
        + points[3][:, 0:1] * press[3:4, :]
    ) * points[0][:, 0:1] * (inverse * inverse)
    for c in range(6):
        at = pl.ds(32 * c, 32)
        value = SHEAR[c] * viscosity * (rates[3, at, :] + direction * rates[2, at, :])
        if c < 3:
            value -= pressure
        high, low = split(value)
        stress[32 * c : 32 * c + 32, :] = high
        stress[192 + 32 * c : 224 + 32 * c, :] = low
        stress[384 + 32 * c : 416 + 32 * c, :] = high
    local[...] = jnp.dot(force[...], stress[...], preferred_element_type=F32)
    for b in range(4):
        faces[b] = local[88:280, 128 * b : 128 * b + 128]
    send(faces.at[3], halo.at[0], halo_send.at[0], halo_recv.at[0], after)
    send(faces.at[0], halo.at[1], halo_send.at[1], halo_recv.at[1], before)

    low_lane = iota((192, 128), 1) < 64

    def window(b):
        last = halo[0] if b == 0 else faces[b - 1]
        following = halo[1] if b == 3 else faces[b + 1]
        beside_high, beside_low = split(jnp.where(low_lane, following, last))
        own_high, own_low = split(faces[b])
        for f in range(6):
            at = slice(32 * f, 32 * f + 32)
            window_rows = jnp.concatenate([
                jnp.concatenate([beside_high[at], own_high[at]], 1),
                jnp.concatenate([beside_low[at], own_low[at]], 1),
            ], 0)
            other = f ^ 1
            got = jnp.dot(window_rows, hits[other, :, 128 * b : 128 * b + 128], preferred_element_type=F32)
            picked[32 * other : 32 * other + 32, 128 * b : 128 * b + 128] = got[0:32].astype(BF16)
            picked[192 + 32 * other : 224 + 32 * other, 128 * b : 128 * b + 128] = got[32:64].astype(BF16)

    window(1)
    window(2)
    drain(halo.at[0], halo_recv.at[0])
    window(0)
    drain(halo.at[1], halo_recv.at[1])
    window(3)
    added = jnp.dot(place[...], picked[...], preferred_element_type=F32)
    res[...] = local[0:81, :] + added[0:81, :]

    drain(side.at[0], side_recv.at[0])
    drain(side.at[1], side_recv.at[1])
    tile = table[0]
    row, lane = iota((8, 128), 0), iota((8, 128), 1)
    up = pltpu.roll(tile, 1, 1)
    up_row = pltpu.roll(up, 1, 0)
    up_side = pltpu.roll(pltpu.roll(side[0], 1, 1), 5, 0)
    up_side = jnp.where(blk == 0, 0.0, up_side)
    prev = jnp.where(lane == 0, jnp.where(row == 4, up_side, up_row), up)
    down = pltpu.roll(tile, 127, 1)
    down_row = pltpu.roll(down, 7, 0)
    down_side = pltpu.roll(pltpu.roll(side[1], 127, 1), 3, 0)
    down_side = jnp.where(blk == nblk - 1, 0.0, down_side)
    following = jnp.where(lane == 127, jnp.where(row == 7, down_side, down_row), down)
    smooth = BETA_REG * (2.0 * tile - prev - following)

    drain(keys.at[pl.ds(0, nz - 1)], key_send)
    drain(table.at[pl.ds(0, ny - 1)], tab_send)
    drain(sums.at[1, pl.ds(0, ny - 1)], sum_send)
    drain(gathered.at[pl.ds(0, nz - 1)], rep_send)
    drain(partial.at[pl.ds(0, nseg - 1)], par_send)
    for i in range(2):
        drain(side.at[i], side_send.at[i])
        drain(halo.at[i], halo_send.at[i])

    drain(partial.at[pl.ds(0, nseg - 1)], par_recv)
    result = partial[0]
    for k in range(1, nseg):
        result += partial[k]
    hess[...] = result + smooth[4:8, :]


def per_device(nz, ny, nseg, tables, *args):
    vel = args[:4]
    press, visc, scale, log_visc, direction, adj, hang, owner = args[4:]
    dma = pltpu.SemaphoreType.DMA
    vmem = pltpu.VMEM
    residual, hessian = pl.pallas_call(
        functools.partial(kernel, nz, ny, nseg),
        out_shape=(pltpu.VMEM((81, 512), F32), pltpu.VMEM((4, 128), F32)),
        in_specs=[pl.BlockSpec(memory_space=pltpu.HBM)] * 16,
        out_specs=(pl.BlockSpec(memory_space=pltpu.VMEM),) * 2,
        scratch_shapes=[
            vmem((4, 81, 512), F32), vmem((4, 512), F32), vmem((27, 512), F32), vmem((1, 512), F32),
            vmem((4, 128), F32), vmem((4, 128), F32), vmem((6, 512), jnp.int32), vmem((6, 512), jnp.int32),
            vmem((1, 512), jnp.int32),
            vmem((192, 256), BF16), vmem((288, 576), BF16), vmem((96, 384), BF16), vmem((4, 32, 128), F32),
            vmem((4, 192, 512), F32),
            vmem((256, 512), BF16),
            vmem((nz, 4, 512), F32),
            vmem((ny, 8, 128), F32),
            vmem((2, 8, 128), F32),
            vmem((nz, 128, 512), BF16),
            vmem((2, ny, 8, 128), F32),
            vmem((nz, 2, 512), F32),
            vmem((nz, 2, 512), F32),
            vmem((nseg, 4, 128), F32),
            vmem((4, 192, 128), F32),
            vmem((2, 192, 128), F32),
            vmem((6, 256, 512), BF16),
            vmem((576, 512), BF16),
            vmem((288, 512), F32),
            vmem((2, 8 * ny, 128), BF16),
            vmem((384, 512), BF16),
            dma((16,)), dma, dma((nz,)), dma, dma, dma((2,)), dma((2,)),
            dma, dma, dma, dma, dma, dma, dma((2,)), dma((2,)),
        ],
        compiler_params=pltpu.CompilerParams(
            collective_id=0, has_side_effects=True, vmem_limit_bytes=32 * 1024 * 1024
        ),
    )(
        *[
            pltpu.with_memory_space_constraint(x, pltpu.HBM)
            for x in (*vel, press, visc, scale.reshape(1, 512), log_visc.reshape(4, 128), direction.reshape(4, 128), adj,
                      hang, owner.reshape(1, 512), *tables)
        ],
    )
    return residual, hessian.reshape(512)


def solution(mesh):
    nseg, nblk = mesh.shape["seg"], mesh.shape["blk"]
    ny = max(d for d in (1, 2, 4, 8) if d * d <= nblk)
    tables = constants()
    octants = P(None, ("seg", "blk"))
    line = P(("seg", "blk"))
    placed = (octants,) * 6 + (line, P("blk"), P("blk"), octants, octants, line)

    def step(*args):
        return per_device(nblk // ny, ny, nseg, [jnp.asarray(t) for t in tables], *args)

    return jax.shard_map(step, mesh=mesh, in_specs=placed, out_specs=(octants, P("blk")), check_vma=False)
```

```python
import functools

import jax
import jax.numpy as jnp
import ml_dtypes
import numpy as np
from jax import lax
from jax.experimental import pallas as pl
from jax.experimental.pallas import tpu as pltpu
from jax.sharding import PartitionSpec as P

MESH = pl.DeviceIdType.MESH
F32 = jnp.float32
BF16 = jnp.bfloat16
BETA_REG = 1.0
SHEAR = (1.0, 1.0, 1.0, 2.0, 2.0, 2.0)


def element_tables():
    gauss = np.array([-np.sqrt(0.6), 0.0, np.sqrt(0.6)])
    weights_one = np.array([5.0 / 9.0, 8.0 / 9.0, 5.0 / 9.0])
    values = np.stack([gauss * (gauss - 1.0) / 2.0, 1.0 - gauss * gauss, gauss * (gauss + 1.0) / 2.0])
    slopes = np.stack([gauss - 0.5, -2.0 * gauss, gauss + 0.5])
    gradient = np.zeros((3, 27, 27))
    for r in range(3):
        parts = [slopes if d == r else values for d in range(3)]
        gradient[r] = np.einsum("ia,jb,kc->abcijk", *parts).reshape(27, 27)
    quad_weight = np.einsum("a,b,c->abc", weights_one, weights_one, weights_one).reshape(27)
    coords = np.stack([g.reshape(27) for g in np.meshgrid(gauss, gauss, gauss, indexing="ij")], 1)
    pairs = [(0, 0), (1, 1), (2, 2), (0, 1), (1, 2), (0, 2)]
    strain = np.zeros((6, 27, 81))
    for comp, (left, right) in enumerate(pairs):
        strain[comp, :, left * 27 : (left + 1) * 27] += 0.5 * gradient[right]
        strain[comp, :, right * 27 : (right + 1) * 27] += 0.5 * gradient[left]
    select = np.zeros((81, 6, 32))
    for face in range(6):
        direction, side = face // 2, 2 * (face % 2)
        nodes = [n for n in range(27) if (n // 9, n // 3 % 3, n % 3)[direction] == side]
        for comp in range(3):
            for place in range(9):
                select[comp * 27 + nodes[place], face, comp * 9 + place] = 1.0
    return strain.astype(np.float32), quad_weight, coords, select


def halves(table):
    high = table.astype(ml_dtypes.bfloat16)
    low = (table - high.astype(np.float32)).astype(ml_dtypes.bfloat16)
    return high, low


def constants():
    strain, quad_weight, coords, select = element_tables()
    padded = np.zeros((6, 32, 81), np.float32)
    padded[:, :27] = strain
    padded = padded.reshape(192, 81)
    high, low = halves(padded)
    rate = np.zeros((192, 256), ml_dtypes.bfloat16)
    rate[:, 0:80], rate[:, 80:160], rate[:, 160:240] = high[:, :80], high[:, :80], low[:, :80]
    rate[:, 240], rate[:, 241], rate[:, 242] = high[:, 80], high[:, 80], low[:, 80]
    rows = np.zeros((288, 192), np.float32)
    rows[:81] = padded.T
    rows[88:280] = select.reshape(81, 192).T @ padded.T
    high, low = halves(rows)
    force = np.concatenate([high, high, low], 1)
    place = np.zeros((96, 384), ml_dtypes.bfloat16)
    place[:81, :192] = select.reshape(81, 192)
    place[:81, 192:] = select.reshape(81, 192)
    points = np.zeros((4, 32, 128), np.float32)
    points[0, :27] = quad_weight[:, None]
    for d in range(3):
        points[d + 1, :27] = coords[:, d, None]
    choose = np.zeros((192, 96), ml_dtypes.bfloat16)
    choose[:, :81] = select.reshape(81, 192).T
    return rate, force, place, points, choose


def split(x):
    high = x.astype(BF16)
    return high, (x - high.astype(F32)).astype(BF16)


def iota(shape, dim):
    return lax.broadcasted_iota(jnp.int32, shape, dim)


def far_first(count, stride):
    return sorted(range(1, count), key=lambda k: -min(k // stride, (count - k) // stride))


def kernel(
    nz, ny, nseg,
    vel_f, vel_i, vel_a, vel_ia, press_h, visc_h, scale_h, log_h, dir_h, adj_h, hang_h, own_h,
    rate_h, force_h, place_h, points_h, choose_h,
    res, hess,
    vel, press, visc, scale, log_v, dir_v, adj, hang, own, rate, force, place, points, choose,
    rates, vstack, keys, table, side, onehot, sums, reply, gathered, partial, packed, halo, hits,
    stress, local, spread, picked,
    load_sem, key_send, key_recv, tab_send, tab_recv, side_send, side_recv,
    sum_send, sum_recv, rep_send, rep_recv, par_send, par_recv, halo_send, halo_recv,
):
    seg, blk = lax.axis_index("seg"), lax.axis_index("blk")
    z, y = blk // ny, lax.rem(blk, ny)
    nblk = nz * ny
    flat = seg * nblk + blk
    total = nseg * nblk
    after, before = lax.rem(flat + 1, total), lax.rem(flat + total - 1, total)
    after, before = (after // nblk, lax.rem(after, nblk)), (before // nblk, lax.rem(before, nblk))
    z_peer = [(seg, lax.rem(z + k, nz) * ny + y) for k in range(nz)]
    y_peer = [(seg, z * ny + lax.rem(y + k, ny)) for k in range(ny)]
    s_peer = [(lax.rem(seg + k, nseg), blk) for k in range(nseg)]

    pairs = [
        (vel_f, vel.at[0]), (vel_i, vel.at[1]), (vel_a, vel.at[2]), (vel_ia, vel.at[3]), (rate_h, rate), (visc_h, visc),
        (scale_h, scale), (own_h, own), (points_h, points), (log_h, log_v), (dir_h, dir_v), (adj_h, adj), (hang_h, hang),
        (force_h, force), (press_h, press), (place_h, place), (choose_h, choose),
    ]
    loads = [pltpu.make_async_copy(a, b, load_sem.at[i]) for i, (a, b) in enumerate(pairs)]
    for load in loads[:5]:
        load.start()

    barrier = pltpu.get_barrier_semaphore()
    peers = [z_peer[k] for k in far_first(nz, 1)] + [s_peer[k] for k in far_first(nseg, 2)]
    peers += [y_peer[k] for k in far_first(ny, 1)] + [after, before]
    for peer in peers:
        pl.semaphore_signal(barrier, inc=1, device_id=peer, device_id_type=MESH)

    for load in loads[5:11]:
        load.start()

    def send(src, dst, send_sem, recv_sem, peer):
        pltpu.make_async_remote_copy(
            src_ref=src, dst_ref=dst, send_sem=send_sem, recv_sem=recv_sem, device_id=peer, device_id_type=MESH
        ).start()

    def drain(ref, sem):
        pltpu.make_async_copy(ref, ref, sem).wait()

    for i in range(4):
        loads[i].wait()
        if i == 0:
            loads[4].wait()
        high, low = split(vel[i, 0:80, :])
        last_high = vel[i, 80:81, :].astype(BF16).astype(F32)
        last_low = vel[i, 80:81, :] - last_high
        row = iota((16, 512), 0)
        tail = jnp.where((row == 0) | (row == 2), last_high, jnp.where(row == 1, last_low, 0.0)).astype(BF16)
        vstack[i, 0:80, :] = high
        vstack[i, 80:160, :] = low
        vstack[i, 160:240, :] = high
        vstack[i, 240:256, :] = tail
        rates[i] = jnp.dot(rate[...], vstack[i], preferred_element_type=F32)

    for i in range(5, 9):
        loads[i].wait()
    inverse = 1.0 / scale[...]
    factor = jnp.concatenate([visc[...], jnp.zeros((5, 512), F32)], 0)
    base = 2.0 * factor * points[0][:, 0:1] * inverse
    first = jnp.zeros((32, 512), F32)
    second = jnp.zeros((32, 512), F32)
    for c in range(6):
        at = pl.ds(32 * c, 32)
        fwd, inc, adjoint, incadj = rates[0, at, :], rates[1, at, :], rates[2, at, :], rates[3, at, :]
        first += SHEAR[c] * (inc * adjoint + fwd * incadj)
        second += SHEAR[c] * (fwd * adjoint)
    sum_first = jnp.sum(base * first, axis=0, keepdims=True)
    sum_second = jnp.sum(base * second, axis=0, keepdims=True)
    owner = own[...]
    row_of = owner // 128
    block_of = row_of // 4
    block_y = lax.rem(block_of, ny)
    slot = lax.rem(y - block_y + ny, ny)
    key = (block_of // ny) * (4 * ny) + slot * 4 + lax.rem(row_of, 4)
    column = lax.rem(owner, 128)
    keys[0, 0:1, :] = key.astype(F32)
    keys[0, 1:2, :] = column.astype(F32)
    keys[0, 2:3, :] = sum_first
    keys[0, 3:4, :] = sum_second
    loads[9].wait()
    loads[10].wait()
    table[0, 0:4, :] = log_v[...]
    table[0, 4:8, :] = dir_v[...]

    pl.semaphore_wait(barrier, len(peers))
    for k in range(1, nz):
        send(keys.at[0], keys.at[k], key_send, key_recv.at[k], z_peer[k])
    for k in range(1, ny):
        send(table.at[0], table.at[k], tab_send, tab_recv, y_peer[k])
    send(table.at[0], side.at[0], side_send.at[0], side_recv.at[0], after)
    send(table.at[0], side.at[1], side_send.at[1], side_recv.at[1], before)

    for load in loads[11:]:
        load.start()
    loads[11].wait()
    loads[12].wait()
    lane = lax.rem(iota((1, 512), 1), 128)
    for f in range(6):
        reach = adj[f : f + 1, :]
        target = lax.rem(lane + reach + 384, 256)
        weight = jnp.where(reach != 0, jnp.where(hang[f : f + 1, :] == 1, 0.25, 1.0), 0.0)
        hits[f] = jnp.where(iota((256, 512), 0) == target, weight, 0.0).astype(BF16)

    rho = iota((8 * ny, 512), 0)
    wanted = (z * (4 * ny) + (rho // 8) * 4 + lax.rem(rho, 4)).astype(F32)
    is_second = lax.rem(rho, 8) >= 4
    acc = jnp.zeros((16 * ny, 128), F32)
    for d in [0] + list(range(nz - 1, 0, -1)):
        if d > 0:
            drain(keys.at[d], key_recv.at[d])
        hit = keys[d, 0:1, :] == wanted
        value = jnp.where(is_second, keys[d, 3:4, :], keys[d, 2:3, :])
        value = jnp.where(hit, value, 0.0)
        high, low = split(value)
        onehot[d] = jnp.where(iota((128, 512), 0).astype(F32) == keys[d, 1:2, :], 1.0, 0.0).astype(BF16)
        acc += lax.dot_general(
            jnp.concatenate([high, low], 0), onehot[d], (((1,), (1,)), ((), ())), preferred_element_type=F32
        )
    dense = acc[0 : 8 * ny, :] + acc[8 * ny : 16 * ny, :]
    for k in range(ny):
        sums[0, k] = dense[8 * k : 8 * k + 8, :]
    for k in far_first(ny, 1):
        send(sums.at[0, k], sums.at[1, k], sum_send, sum_recv, y_peer[ny - k])

    drain(table.at[pl.ds(0, ny - 1)], tab_recv)
    rows = [
        jnp.concatenate([table[k, 4 * part : 4 * part + 4, :] for k in range(ny)], 0) for part in range(2)
    ]
    high, low = split(jnp.concatenate(rows, 1).T)
    spread[...] = jnp.concatenate([high, low], 1)
    key_row = (z * (4 * ny) + lax.rem(iota((8 * ny, 512), 0), 4 * ny)).astype(F32)
    for d in far_first(nz, 1) + [0]:
        pick = jnp.where(keys[d, 0:1, :] == key_row, 1.0, 0.0).astype(BF16)
        mask = onehot[d].astype(F32)
        found = jnp.dot(spread[...], pick, preferred_element_type=F32)
        reply[d, 0:1, :] = jnp.sum(found[0:128] * mask, axis=0, keepdims=True)
        reply[d, 1:2, :] = jnp.sum(found[128:256] * mask, axis=0, keepdims=True)
        if d > 0:
            send(reply.at[d], gathered.at[d], rep_send, rep_recv, z_peer[nz - d])

    owned = jnp.exp(table[0, 0:4, :])
    drain(sums.at[1, pl.ds(0, ny - 1)], sum_recv)
    mine = sums[0, 0]
    for k in range(1, ny):
        mine += sums[1, k]
    share = owned * (mine[0:4, :] + table[0, 4:8, :] * mine[4:8, :])
    partial[seg] = share
    for k in far_first(nseg, 2):
        send(partial.at[seg], partial.at[seg], par_send, par_recv, s_peer[k])

    drain(gathered.at[pl.ds(0, nz - 1)], rep_recv)
    found = reply[0]
    for k in range(1, nz):
        found += gathered[k]
    viscosity = jnp.exp(found[0:1, :]) * base
    direction = found[1:2, :]
    for i in range(13, 17):
        loads[i].wait()
    pressure = (
        press[0:1, :] + points[1][:, 0:1] * press[1:2, :] + points[2][:, 0:1] * press[2:3, :]
        + points[3][:, 0:1] * press[3:4, :]
    ) * points[0][:, 0:1] * (inverse * inverse)
    low_lane = iota((48, 128), 1) < 64
    for columns in (slice(384, 512), slice(0, 128), slice(128, 384)):
        for c in range(6):
            at = pl.ds(32 * c, 32)
            value = SHEAR[c] * viscosity[:, columns] * (
                rates[3, at, columns] + direction[:, columns] * rates[2, at, columns]
            )
            if c < 3:
                value -= pressure[:, columns]
            high, low = split(value)
            stress[32 * c : 32 * c + 32, columns] = high
            stress[192 + 32 * c : 224 + 32 * c, columns] = low
            stress[384 + 32 * c : 416 + 32 * c, columns] = high
        local[:, columns] = jnp.dot(force[...], stress[:, columns], preferred_element_type=F32)
        if columns.start == 384:
            packed[0] = jnp.where(low_lane, pltpu.roll(local[0:48, columns], 64, 1), local[48:96, columns])
            send(packed.at[0], halo.at[0], halo_send.at[0], halo_recv.at[0], after)
        if columns.start == 0:
            packed[1] = jnp.where(low_lane, local[0:48, columns], pltpu.roll(local[48:96, columns], 64, 1))
            send(packed.at[1], halo.at[1], halo_send.at[1], halo_recv.at[1], before)

    low_lane = iota((192, 128), 1) < 64

    def halo_faces(rows):
        high, low = split(jnp.concatenate(rows, 0))
        return [jnp.dot(choose[...], part, preferred_element_type=F32) for part in (high, low)]

    def own_faces(b):
        return [part.astype(F32) for part in split(local[88:280, 128 * b : 128 * b + 128])]

    def window(b):
        if b == 0:
            last = halo_faces([pltpu.roll(halo[0], 64, 1), halo[0]])
        else:
            last = own_faces(b - 1)
        if b == 3:
            following = halo_faces([halo[1], pltpu.roll(halo[1], 64, 1)])
        else:
            following = own_faces(b + 1)
        beside_high, beside_low = [jnp.where(low_lane, n, p).astype(BF16) for n, p in zip(following, last)]
        own_high, own_low = split(local[88:280, 128 * b : 128 * b + 128])
        for f in range(6):
            at = slice(32 * f, 32 * f + 32)
            window_rows = jnp.concatenate([
                jnp.concatenate([beside_high[at], own_high[at]], 1),
                jnp.concatenate([beside_low[at], own_low[at]], 1),
            ], 0)
            other = f ^ 1
            got = jnp.dot(window_rows, hits[other, :, 128 * b : 128 * b + 128], preferred_element_type=F32)
            picked[32 * other : 32 * other + 32, 128 * b : 128 * b + 128] = got[0:32].astype(BF16)
            picked[192 + 32 * other : 224 + 32 * other, 128 * b : 128 * b + 128] = got[32:64].astype(BF16)

    def settle(columns):
        added = jnp.dot(place[...], picked[:, columns], preferred_element_type=F32)
        res[:, columns] = local[0:81, columns] + added[0:81, :]

    window(1)
    window(2)
    settle(slice(128, 384))
    drain(halo.at[1], halo_recv.at[1])
    window(3)
    settle(slice(384, 512))

    drain(side.at[0], side_recv.at[0])
    drain(side.at[1], side_recv.at[1])
    tile = table[0]
    row, lane = iota((8, 128), 0), iota((8, 128), 1)
    up = pltpu.roll(tile, 1, 1)
    up_row = pltpu.roll(up, 1, 0)
    up_side = pltpu.roll(pltpu.roll(side[0], 1, 1), 5, 0)
    up_side = jnp.where(blk == 0, 0.0, up_side)
    prev = jnp.where(lane == 0, jnp.where(row == 4, up_side, up_row), up)
    down = pltpu.roll(tile, 127, 1)
    down_row = pltpu.roll(down, 7, 0)
    down_side = pltpu.roll(pltpu.roll(side[1], 127, 1), 3, 0)
    down_side = jnp.where(blk == nblk - 1, 0.0, down_side)
    following = jnp.where(lane == 127, jnp.where(row == 7, down_side, down_row), down)
    smooth = BETA_REG * (2.0 * tile - prev - following)

    drain(keys.at[pl.ds(0, nz - 1)], key_send)
    drain(table.at[pl.ds(0, ny - 1)], tab_send)
    drain(sums.at[1, pl.ds(0, ny - 1)], sum_send)
    drain(gathered.at[pl.ds(0, nz - 1)], rep_send)
    drain(partial.at[pl.ds(0, nseg - 1)], par_send)
    for i in range(2):
        drain(side.at[i], side_send.at[i])
        drain(halo.at[i], halo_send.at[i])

    drain(halo.at[0], halo_recv.at[0])
    window(0)
    settle(slice(0, 128))

    drain(partial.at[pl.ds(0, nseg - 1)], par_recv)
    result = partial[0]
    for k in range(1, nseg):
        result += partial[k]
    hess[...] = result + smooth[4:8, :]


def deliver(res_in, hess_in, res_out, hess_out, sem):
    copies = [
        pltpu.make_async_copy(res_in, res_out, sem.at[0]),
        pltpu.make_async_copy(hess_in, hess_out, sem.at[1]),
    ]
    for copy in copies:
        copy.start()
    for copy in copies:
        copy.wait()


def per_device(nz, ny, nseg, tables, *args):
    vel = args[:4]
    press, visc, scale, log_visc, direction, adj, hang, owner = args[4:]
    dma = pltpu.SemaphoreType.DMA
    vmem = pltpu.VMEM
    residual, hessian = pl.pallas_call(
        functools.partial(kernel, nz, ny, nseg),
        out_shape=(pltpu.VMEM((81, 512), F32), pltpu.VMEM((4, 128), F32)),
        in_specs=[pl.BlockSpec(memory_space=pltpu.HBM)] * 17,
        out_specs=(pl.BlockSpec(memory_space=pltpu.VMEM),) * 2,
        scratch_shapes=[
            vmem((4, 81, 512), F32), vmem((4, 512), F32), vmem((27, 512), F32), vmem((1, 512), F32),
            vmem((4, 128), F32), vmem((4, 128), F32), vmem((6, 512), jnp.int32), vmem((6, 512), jnp.int32),
            vmem((1, 512), jnp.int32),
            vmem((192, 256), BF16), vmem((288, 576), BF16), vmem((96, 384), BF16), vmem((4, 32, 128), F32), vmem((192, 96), BF16),
            vmem((4, 192, 512), F32),
            vmem((4, 256, 512), BF16),
            vmem((nz, 4, 512), F32),
            vmem((ny, 8, 128), F32),
            vmem((2, 8, 128), F32),
            vmem((nz, 128, 512), BF16),
            vmem((2, ny, 8, 128), F32),
            vmem((nz, 2, 512), F32),
            vmem((nz, 2, 512), F32),
            vmem((nseg, 4, 128), F32),
            vmem((2, 48, 128), F32),
            vmem((2, 48, 128), F32),
            vmem((6, 256, 512), BF16),
            vmem((576, 512), BF16),
            vmem((288, 512), F32),
            vmem((256, 8 * ny), BF16),
            vmem((384, 512), BF16),
            dma((17,)), dma, dma((nz,)), dma, dma, dma((2,)), dma((2,)),
            dma, dma, dma, dma, dma, dma, dma((2,)), dma((2,)),
        ],
        compiler_params=pltpu.CompilerParams(
            collective_id=0, has_side_effects=True, vmem_limit_bytes=32 * 1024 * 1024
        ),
    )(
        *[
            pltpu.with_memory_space_constraint(x, pltpu.HBM)
            for x in (*vel, press, visc, scale.reshape(1, 512), log_visc.reshape(4, 128), direction.reshape(4, 128), adj,
                      hang, owner.reshape(1, 512), *tables)
        ],
    )
    residual, hessian = pl.pallas_call(
        deliver,
        out_shape=(jax.ShapeDtypeStruct((81, 512), F32), jax.ShapeDtypeStruct((4, 128), F32)),
        in_specs=[pl.BlockSpec(memory_space=pltpu.VMEM)] * 2,
        out_specs=(pl.BlockSpec(memory_space=pl.ANY),) * 2,
        scratch_shapes=[dma((2,))],
    )(*[pltpu.with_memory_space_constraint(x, pltpu.VMEM) for x in (residual, hessian)])
    return residual, hessian.reshape(512)


def solution(mesh):
    nseg, nblk = mesh.shape["seg"], mesh.shape["blk"]
    ny = max(d for d in (1, 2, 4, 8) if d * d <= nblk)
    tables = constants()
    octants = P(None, ("seg", "blk"))
    line = P(("seg", "blk"))
    placed = (octants,) * 6 + (line, P("blk"), P("blk"), octants, octants, line)

    def step(*args):
        return per_device(nblk // ny, ny, nseg, [jnp.asarray(t) for t in tables], *args)

    return jax.shard_map(step, mesh=mesh, in_specs=placed, out_specs=(octants, P("blk")), check_vma=False)
```

```python
import functools

import jax
import jax.numpy as jnp
import ml_dtypes
import numpy as np
from jax import lax
from jax.experimental import pallas as pl
from jax.experimental.pallas import tpu as pltpu
from jax.sharding import PartitionSpec as P

MESH = pl.DeviceIdType.MESH
F32 = jnp.float32
BF16 = jnp.bfloat16
BETA_REG = 1.0
SHEAR = (1.0, 1.0, 1.0, 2.0, 2.0, 2.0)


def element_tables():
    gauss = np.array([-np.sqrt(0.6), 0.0, np.sqrt(0.6)])
    weights_one = np.array([5.0 / 9.0, 8.0 / 9.0, 5.0 / 9.0])
    values = np.stack([gauss * (gauss - 1.0) / 2.0, 1.0 - gauss * gauss, gauss * (gauss + 1.0) / 2.0])
    slopes = np.stack([gauss - 0.5, -2.0 * gauss, gauss + 0.5])
    gradient = np.zeros((3, 27, 27))
    for r in range(3):
        parts = [slopes if d == r else values for d in range(3)]
        gradient[r] = np.einsum("ia,jb,kc->abcijk", *parts).reshape(27, 27)
    quad_weight = np.einsum("a,b,c->abc", weights_one, weights_one, weights_one).reshape(27)
    coords = np.stack([g.reshape(27) for g in np.meshgrid(gauss, gauss, gauss, indexing="ij")], 1)
    pairs = [(0, 0), (1, 1), (2, 2), (0, 1), (1, 2), (0, 2)]
    strain = np.zeros((6, 27, 81))
    for comp, (left, right) in enumerate(pairs):
        strain[comp, :, left * 27 : (left + 1) * 27] += 0.5 * gradient[right]
        strain[comp, :, right * 27 : (right + 1) * 27] += 0.5 * gradient[left]
    select = np.zeros((81, 6, 32))
    for face in range(6):
        direction, side = face // 2, 2 * (face % 2)
        nodes = [n for n in range(27) if (n // 9, n // 3 % 3, n % 3)[direction] == side]
        for comp in range(3):
            for place in range(9):
                select[comp * 27 + nodes[place], face, comp * 9 + place] = 1.0
    return strain.astype(np.float32), quad_weight, coords, select


def halves(table):
    high = table.astype(ml_dtypes.bfloat16)
    low = (table - high.astype(np.float32)).astype(ml_dtypes.bfloat16)
    return high, low


def constants():
    strain, quad_weight, coords, select = element_tables()
    padded = np.zeros((6, 32, 81), np.float32)
    padded[:, :27] = strain
    padded = padded.reshape(192, 81)
    high, low = halves(padded)
    rate = np.zeros((192, 256), ml_dtypes.bfloat16)
    rate[:, 0:80], rate[:, 80:160], rate[:, 160:240] = high[:, :80], high[:, :80], low[:, :80]
    rate[:, 240], rate[:, 241], rate[:, 242] = high[:, 80], high[:, 80], low[:, 80]
    rows = np.zeros((288, 192), np.float32)
    rows[:81] = padded.T
    rows[88:280] = select.reshape(81, 192).T @ padded.T
    high, low = halves(rows)
    force = np.concatenate([high, high, low], 1)
    place = np.zeros((96, 384), ml_dtypes.bfloat16)
    place[:81, :192] = select.reshape(81, 192)
    place[:81, 192:] = select.reshape(81, 192)
    points = np.zeros((4, 32, 128), np.float32)
    points[0, :27] = quad_weight[:, None]
    for d in range(3):
        points[d + 1, :27] = coords[:, d, None]
    choose = np.zeros((192, 96), ml_dtypes.bfloat16)
    choose[:, :81] = select.reshape(81, 192).T
    return rate, force, place, points, choose


def split(x):
    high = x.astype(BF16)
    return high, (x - high.astype(F32)).astype(BF16)


def iota(shape, dim):
    return lax.broadcasted_iota(jnp.int32, shape, dim)


def far_first(count, stride):
    return sorted(range(1, count), key=lambda k: -min(k // stride, (count - k) // stride))


def kernel(
    nz, ny, nseg,
    vel_f, vel_i, vel_a, vel_ia, press_h, visc_h, scale_h, log_h, dir_h, adj_h, hang_h, own_h,
    rate_h, force_h, place_h, points_h, choose_h,
    res, hess,
    vel, press, visc, scale, log_v, dir_v, adj, hang, own, rate, force, place, points, choose,
    rates, vstack, keys, table, side, onehot, sums, reply, gathered, partial, packed, halo, hits,
    stress, local, spread, picked,
    load_sem, key_send, key_recv, tab_send, tab_recv, side_send, side_recv,
    sum_send, sum_recv, rep_send, rep_recv, par_send, par_recv, halo_send, halo_recv,
):
    seg, blk = lax.axis_index("seg"), lax.axis_index("blk")
    z, y = blk // ny, lax.rem(blk, ny)
    nblk = nz * ny
    flat = seg * nblk + blk
    total = nseg * nblk
    after, before = lax.rem(flat + 1, total), lax.rem(flat + total - 1, total)
    after, before = (after // nblk, lax.rem(after, nblk)), (before // nblk, lax.rem(before, nblk))
    z_peer = [(seg, lax.rem(z + k, nz) * ny + y) for k in range(nz)]
    y_peer = [(seg, z * ny + lax.rem(y + k, ny)) for k in range(ny)]
    s_peer = [(lax.rem(seg + k, nseg), blk) for k in range(nseg)]

    pairs = [
        (vel_f, vel.at[0]), (vel_i, vel.at[1]), (vel_a, vel.at[2]), (vel_ia, vel.at[3]), (rate_h, rate), (visc_h, visc),
        (scale_h, scale), (own_h, own), (points_h, points), (log_h, log_v), (dir_h, dir_v), (adj_h, adj), (hang_h, hang),
        (force_h, force), (press_h, press), (place_h, place), (choose_h, choose),
    ]
    loads = [pltpu.make_async_copy(a, b, load_sem.at[i]) for i, (a, b) in enumerate(pairs)]
    for load in loads[:5]:
        load.start()

    barrier = pltpu.get_barrier_semaphore()
    far_s = far_first(nseg, 2)
    peers = [s_peer[k] for k in far_s[:3]] + [z_peer[k] for k in far_first(nz, 1)] + [s_peer[k] for k in far_s[3:]]
    peers += [y_peer[k] for k in far_first(ny, 1)] + [after, before]
    for peer in peers:
        pl.semaphore_signal(barrier, inc=1, device_id=peer, device_id_type=MESH)

    for load in loads[5:11]:
        load.start()

    def send(src, dst, send_sem, recv_sem, peer):
        pltpu.make_async_remote_copy(
            src_ref=src, dst_ref=dst, send_sem=send_sem, recv_sem=recv_sem, device_id=peer, device_id_type=MESH
        ).start()

    def drain(ref, sem):
        pltpu.make_async_copy(ref, ref, sem).wait()

    for i in range(4):
        loads[i].wait()
        if i == 0:
            loads[4].wait()
        high, low = split(vel[i, 0:80, :])
        last_high = vel[i, 80:81, :].astype(BF16).astype(F32)
        last_low = vel[i, 80:81, :] - last_high
        row = iota((16, 512), 0)
        tail = jnp.where((row == 0) | (row == 2), last_high, jnp.where(row == 1, last_low, 0.0)).astype(BF16)
        vstack[i, 0:80, :] = high
        vstack[i, 80:160, :] = low
        vstack[i, 160:240, :] = high
        vstack[i, 240:256, :] = tail
        rates[i] = jnp.dot(rate[...], vstack[i], preferred_element_type=F32)

    for i in range(5, 9):
        loads[i].wait()
    inverse = 1.0 / scale[...]
    factor = jnp.concatenate([visc[...], jnp.zeros((5, 512), F32)], 0)
    base = 2.0 * factor * points[0][:, 0:1] * inverse
    first = jnp.zeros((32, 512), F32)
    second = jnp.zeros((32, 512), F32)
    for c in range(6):
        at = pl.ds(32 * c, 32)
        fwd, inc, adjoint, incadj = rates[0, at, :], rates[1, at, :], rates[2, at, :], rates[3, at, :]
        first += SHEAR[c] * (inc * adjoint + fwd * incadj)
        second += SHEAR[c] * (fwd * adjoint)
    sum_first = jnp.sum(base * first, axis=0, keepdims=True)
    sum_second = jnp.sum(base * second, axis=0, keepdims=True)
    owner = own[...]
    row_of = owner // 128
    block_of = row_of // 4
    block_y = lax.rem(block_of, ny)
    slot = lax.rem(y - block_y + ny, ny)
    key = (block_of // ny) * (4 * ny) + slot * 4 + lax.rem(row_of, 4)
    column = lax.rem(owner, 128)
    keys[0, 0:1, :] = key.astype(F32)
    keys[0, 1:2, :] = column.astype(F32)
    keys[0, 2:3, :] = sum_first
    keys[0, 3:4, :] = sum_second
    loads[9].wait()
    loads[10].wait()
    table[0, 0:4, :] = log_v[...]
    table[0, 4:8, :] = dir_v[...]

    pl.semaphore_wait(barrier, len(peers))
    for k in range(1, nz):
        send(keys.at[0], keys.at[k], key_send, key_recv.at[k], z_peer[k])
    for k in range(1, ny):
        send(table.at[0], table.at[k], tab_send, tab_recv, y_peer[k])
    send(table.at[0], side.at[0], side_send.at[0], side_recv.at[0], after)
    send(table.at[0], side.at[1], side_send.at[1], side_recv.at[1], before)

    for load in loads[11:]:
        load.start()
    loads[11].wait()
    loads[12].wait()
    lane = lax.rem(iota((1, 512), 1), 128)
    for f in range(6):
        reach = adj[f : f + 1, :]
        target = lax.rem(lane + reach + 384, 256)
        weight = jnp.where(reach != 0, jnp.where(hang[f : f + 1, :] == 1, 0.25, 1.0), 0.0)
        hits[f] = jnp.where(iota((256, 512), 0) == target, weight, 0.0).astype(BF16)

    rho = iota((8 * ny, 512), 0)
    wanted = (z * (4 * ny) + (rho // 8) * 4 + lax.rem(rho, 4)).astype(F32)
    is_second = lax.rem(rho, 8) >= 4
    acc = jnp.zeros((16 * ny, 128), F32)
    for d in [0] + list(range(nz - 1, 0, -1)):
        if d > 0:
            drain(keys.at[d], key_recv.at[d])
        hit = keys[d, 0:1, :] == wanted
        value = jnp.where(is_second, keys[d, 3:4, :], keys[d, 2:3, :])
        value = jnp.where(hit, value, 0.0)
        high, low = split(value)
        onehot[d] = jnp.where(iota((128, 512), 0).astype(F32) == keys[d, 1:2, :], 1.0, 0.0).astype(BF16)
        acc += lax.dot_general(
            jnp.concatenate([high, low], 0), onehot[d], (((1,), (1,)), ((), ())), preferred_element_type=F32
        )
    dense = acc[0 : 8 * ny, :] + acc[8 * ny : 16 * ny, :]
    for k in range(ny):
        sums[0, k] = dense[8 * k : 8 * k + 8, :]
    for k in far_first(ny, 1):
        send(sums.at[0, k], sums.at[1, k], sum_send, sum_recv, y_peer[ny - k])

    drain(table.at[pl.ds(0, ny - 1)], tab_recv)
    rows = [
        jnp.concatenate([table[k, 4 * part : 4 * part + 4, :] for k in range(ny)], 0) for part in range(2)
    ]
    high, low = split(jnp.concatenate(rows, 1).T)
    spread[...] = jnp.concatenate([high, low], 1)
    key_row = (z * (4 * ny) + lax.rem(iota((8 * ny, 512), 0), 4 * ny)).astype(F32)
    for d in far_first(nz, 1) + [0]:
        pick = jnp.where(keys[d, 0:1, :] == key_row, 1.0, 0.0).astype(BF16)
        mask = onehot[d].astype(F32)
        found = jnp.dot(spread[...], pick, preferred_element_type=F32)
        reply[d, 0:1, :] = jnp.sum(found[0:128] * mask, axis=0, keepdims=True)
        reply[d, 1:2, :] = jnp.sum(found[128:256] * mask, axis=0, keepdims=True)
        if d > 0:
            send(reply.at[d], gathered.at[d], rep_send, rep_recv, z_peer[nz - d])

    owned = jnp.exp(table[0, 0:4, :])
    drain(sums.at[1, pl.ds(0, ny - 1)], sum_recv)
    mine = sums[0, 0]
    for k in range(1, ny):
        mine += sums[1, k]
    share = owned * (mine[0:4, :] + table[0, 4:8, :] * mine[4:8, :])
    partial[seg] = share
    in_turn = far_first(nseg, 2)
    for k in in_turn[:10]:
        send(partial.at[seg], partial.at[seg], par_send, par_recv, s_peer[k])

    drain(gathered.at[pl.ds(0, nz - 1)], rep_recv)
    found = reply[0]
    for k in range(1, nz):
        found += gathered[k]
    viscosity = jnp.exp(found[0:1, :]) * base
    direction = found[1:2, :]
    for i in range(13, 17):
        loads[i].wait()
    pressure = (
        press[0:1, :] + points[1][:, 0:1] * press[1:2, :] + points[2][:, 0:1] * press[2:3, :]
        + points[3][:, 0:1] * press[3:4, :]
    ) * points[0][:, 0:1] * (inverse * inverse)
    low_lane = iota((48, 128), 1) < 64
    for columns in (slice(384, 512), slice(0, 128), slice(128, 384)):
        for c in range(6):
            at = pl.ds(32 * c, 32)
            value = SHEAR[c] * viscosity[:, columns] * (
                rates[3, at, columns] + direction[:, columns] * rates[2, at, columns]
            )
            if c < 3:
                value -= pressure[:, columns]
            high, low = split(value)
            stress[32 * c : 32 * c + 32, columns] = high
            stress[192 + 32 * c : 224 + 32 * c, columns] = low
            stress[384 + 32 * c : 416 + 32 * c, columns] = high
        local[:, columns] = jnp.dot(force[...], stress[:, columns], preferred_element_type=F32)
        if columns.start == 384:
            packed[0] = jnp.where(low_lane, pltpu.roll(local[0:48, columns], 64, 1), local[48:96, columns])
            send(packed.at[0], halo.at[0], halo_send.at[0], halo_recv.at[0], after)
        if columns.start == 0:
            packed[1] = jnp.where(low_lane, local[0:48, columns], pltpu.roll(local[48:96, columns], 64, 1))
            send(packed.at[1], halo.at[1], halo_send.at[1], halo_recv.at[1], before)

    for k in in_turn[10:]:
        send(partial.at[seg], partial.at[seg], par_send, par_recv, s_peer[k])
    low_lane = iota((192, 128), 1) < 64

    def halo_faces(rows):
        high, low = split(jnp.concatenate(rows, 0))
        return [jnp.dot(choose[...], part, preferred_element_type=F32) for part in (high, low)]

    def own_faces(b):
        return [part.astype(F32) for part in split(local[88:280, 128 * b : 128 * b + 128])]

    def window(b):
        if b == 0:
            last = halo_faces([pltpu.roll(halo[0], 64, 1), halo[0]])
        else:
            last = own_faces(b - 1)
        if b == 3:
            following = halo_faces([halo[1], pltpu.roll(halo[1], 64, 1)])
        else:
            following = own_faces(b + 1)
        beside_high, beside_low = [jnp.where(low_lane, n, p).astype(BF16) for n, p in zip(following, last)]
        own_high, own_low = split(local[88:280, 128 * b : 128 * b + 128])
        for f in range(6):
            at = slice(32 * f, 32 * f + 32)
            window_rows = jnp.concatenate([
                jnp.concatenate([beside_high[at], own_high[at]], 1),
                jnp.concatenate([beside_low[at], own_low[at]], 1),
            ], 0)
            other = f ^ 1
            got = jnp.dot(window_rows, hits[other, :, 128 * b : 128 * b + 128], preferred_element_type=F32)
            picked[32 * other : 32 * other + 32, 128 * b : 128 * b + 128] = got[0:32].astype(BF16)
            picked[192 + 32 * other : 224 + 32 * other, 128 * b : 128 * b + 128] = got[32:64].astype(BF16)

    def settle(columns):
        added = jnp.dot(place[...], picked[:, columns], preferred_element_type=F32)
        res[:, columns] = local[0:81, columns] + added[0:81, :]

    window(1)
    window(2)
    settle(slice(128, 384))
    drain(halo.at[1], halo_recv.at[1])
    window(3)
    settle(slice(384, 512))

    drain(side.at[0], side_recv.at[0])
    drain(side.at[1], side_recv.at[1])
    tile = table[0]
    row, lane = iota((8, 128), 0), iota((8, 128), 1)
    up = pltpu.roll(tile, 1, 1)
    up_row = pltpu.roll(up, 1, 0)
    up_side = pltpu.roll(pltpu.roll(side[0], 1, 1), 5, 0)
    up_side = jnp.where(blk == 0, 0.0, up_side)
    prev = jnp.where(lane == 0, jnp.where(row == 4, up_side, up_row), up)
    down = pltpu.roll(tile, 127, 1)
    down_row = pltpu.roll(down, 7, 0)
    down_side = pltpu.roll(pltpu.roll(side[1], 127, 1), 3, 0)
    down_side = jnp.where(blk == nblk - 1, 0.0, down_side)
    following = jnp.where(lane == 127, jnp.where(row == 7, down_side, down_row), down)
    smooth = BETA_REG * (2.0 * tile - prev - following)

    drain(halo.at[0], halo_recv.at[0])
    window(0)
    settle(slice(0, 128))

    drain(partial.at[pl.ds(0, nseg - 1)], par_recv)
    result = partial[0]
    for k in range(1, nseg):
        result += partial[k]
    hess[...] = result + smooth[4:8, :]

    drain(keys.at[pl.ds(0, nz - 1)], key_send)
    drain(table.at[pl.ds(0, ny - 1)], tab_send)
    drain(sums.at[1, pl.ds(0, ny - 1)], sum_send)
    drain(gathered.at[pl.ds(0, nz - 1)], rep_send)
    drain(partial.at[pl.ds(0, nseg - 1)], par_send)
    for i in range(2):
        drain(side.at[i], side_send.at[i])
        drain(halo.at[i], halo_send.at[i])


def deliver(res_in, hess_in, res_out, hess_out, sem):
    copies = [
        pltpu.make_async_copy(res_in, res_out, sem.at[0]),
        pltpu.make_async_copy(hess_in, hess_out, sem.at[1]),
    ]
    for copy in copies:
        copy.start()
    for copy in copies:
        copy.wait()


def per_device(nz, ny, nseg, tables, *args):
    vel = args[:4]
    press, visc, scale, log_visc, direction, adj, hang, owner = args[4:]
    dma = pltpu.SemaphoreType.DMA
    vmem = pltpu.VMEM
    residual, hessian = pl.pallas_call(
        functools.partial(kernel, nz, ny, nseg),
        out_shape=(pltpu.VMEM((81, 512), F32), pltpu.VMEM((4, 128), F32)),
        in_specs=[pl.BlockSpec(memory_space=pltpu.HBM)] * 17,
        out_specs=(pl.BlockSpec(memory_space=pltpu.VMEM),) * 2,
        scratch_shapes=[
            vmem((4, 81, 512), F32), vmem((4, 512), F32), vmem((27, 512), F32), vmem((1, 512), F32),
            vmem((4, 128), F32), vmem((4, 128), F32), vmem((6, 512), jnp.int32), vmem((6, 512), jnp.int32),
            vmem((1, 512), jnp.int32),
            vmem((192, 256), BF16), vmem((288, 576), BF16), vmem((96, 384), BF16), vmem((4, 32, 128), F32), vmem((192, 96), BF16),
            vmem((4, 192, 512), F32),
            vmem((4, 256, 512), BF16),
            vmem((nz, 4, 512), F32),
            vmem((ny, 8, 128), F32),
            vmem((2, 8, 128), F32),
            vmem((nz, 128, 512), BF16),
            vmem((2, ny, 8, 128), F32),
            vmem((nz, 2, 512), F32),
            vmem((nz, 2, 512), F32),
            vmem((nseg, 4, 128), F32),
            vmem((2, 48, 128), F32),
            vmem((2, 48, 128), F32),
            vmem((6, 256, 512), BF16),
            vmem((576, 512), BF16),
            vmem((288, 512), F32),
            vmem((256, 8 * ny), BF16),
            vmem((384, 512), BF16),
            dma((17,)), dma, dma((nz,)), dma, dma, dma((2,)), dma((2,)),
            dma, dma, dma, dma, dma, dma, dma((2,)), dma((2,)),
        ],
        compiler_params=pltpu.CompilerParams(
            collective_id=0, has_side_effects=True, vmem_limit_bytes=32 * 1024 * 1024
        ),
    )(
        *[
            pltpu.with_memory_space_constraint(x, pltpu.HBM)
            for x in (*vel, press, visc, scale.reshape(1, 512), log_visc.reshape(4, 128), direction.reshape(4, 128), adj,
                      hang, owner.reshape(1, 512), *tables)
        ],
    )
    residual, hessian = pl.pallas_call(
        deliver,
        out_shape=(jax.ShapeDtypeStruct((81, 512), F32), jax.ShapeDtypeStruct((4, 128), F32)),
        in_specs=[pl.BlockSpec(memory_space=pltpu.VMEM)] * 2,
        out_specs=(pl.BlockSpec(memory_space=pl.ANY),) * 2,
        scratch_shapes=[dma((2,))],
    )(*[pltpu.with_memory_space_constraint(x, pltpu.VMEM) for x in (residual, hessian)])
    return residual, hessian.reshape(512)


def solution(mesh):
    nseg, nblk = mesh.shape["seg"], mesh.shape["blk"]
    ny = max(d for d in (1, 2, 4, 8) if d * d <= nblk)
    tables = constants()
    octants = P(None, ("seg", "blk"))
    line = P(("seg", "blk"))
    placed = (octants,) * 6 + (line, P("blk"), P("blk"), octants, octants, line)

    def step(*args):
        return per_device(nblk // ny, ny, nseg, [jnp.asarray(t) for t in tables], *args)

    return jax.shard_map(step, mesh=mesh, in_specs=placed, out_specs=(octants, P("blk")), check_vma=False)
```
